32 devices in a mesh: parts: 1, local: 32 (over z, y, x, core).
Axes of the slice: x: 2, y: 2, z: 4, core: 2. Of those that a mesh axis runs over, the one named last changes fastest.
Arguments:
- tokens: bfloat16 [256, 7168], P(('parts', 'local')), may hold values from -6 to 6
- routes: int32 [256, 2], P(('parts', 'local')), may hold values from 0 to 3, all different within a row; in each aligned block of 8 rows (0 to 7, 8 to 15, ...) at most 8 rows name the same one
- route_weight: float32 [256, 2], P(('parts', 'local')), may hold values from 0.25 to 1
- gate_weight: bfloat16 [32, 7168, 256], P('local'), may hold values from -0.0625 to 0.0625
- up_weight: bfloat16 [32, 7168, 256], P('local'), may hold values from -0.0625 to 0.0625
- down_weight: bfloat16 [32, 256, 7168], P('local'), may hold values from -0.125 to 0.125
Outputs:
- mixed: bfloat16 [256, 7168], P(('parts', 'local'))
The draws below stay inside these ranges and needn't reach their ends.
Inputs may be any that keep to these rules, and one draw needn't show every extreme that they name: `routes`: among the rows of one device no expert is named by more than 8 rows, a bound that some block reaches.
All inputs are finite; a program needn't handle non-finite values.
Results may differ from the reference program's by a relative error of at most 0.0051.
Values may be sent and summed in bfloat16 or wider, within the bound.
No kernel may reach another device: no remote copies, remote signals or barrier semaphores. Data moves between devices by JAX's collectives and lax.ppermute only.
A program may use at most 128 MiB of HBM per device.

```python
import math
import jax
import jax.numpy as jnp
import numpy as np
from jax import lax

D = 7168
FF = 2048
SPLIT = 8
TOPK = 2
TOK_DEV = 8
HID = 256
EXPERTS = 4
CAP = 8
TOKENS = 256
N_LOCAL = 32


def steps_of(own_key, shape, split, smallest, top_value):
    gain, own = 1.0, jax.random.fold_in(own_key, 6)
    for axis_at, shards_of in split:
        draws = jnp.exp(jax.random.uniform(jax.random.fold_in(own, axis_at), (shards_of,), jnp.float32, smallest / len(split), top_value / len(split)))
        gain = gain * jnp.repeat(draws, shape[axis_at] // shards_of).reshape([-1 if axis == axis_at else 1 for axis in range(len(shape))])
    return gain


def routed_block(rng, own, number, rows, amount, top, bound, lean):
    ranking = jax.random.permutation(rng, amount)
    crowded, usual = portions_of(amount, rows * top, bound, lean, True), portions_of(amount, rows * top, bound, lean, False)
    places = jnp.arange(amount)

    def named(lengths, rotation):
        used = int((lengths > 0).sum())
        fixed = max(1, used // 4)
        moved = fixed + (places - fixed + rotation * (used - fixed)) % max(1, amount - fixed)
        return jnp.zeros((amount,), jnp.int32).at[ranking[jnp.where(places < fixed, places, moved)]].set(jnp.asarray(lengths, jnp.int32))

    lengths = jnp.where(number % 4 == 0, named(crowded, number // 4), named(usual, number - number // 4 - 1))
    mixed = jax.random.permutation(jax.random.fold_in(own, 3), amount)
    source_of, taker = mixed[0:amount // 2 * 2:2], mixed[1:amount // 2 * 2:2]
    margin = jnp.minimum(lengths[source_of] - 1, bound - lengths[taker]) // 2
    margin = jnp.where((source_of == ranking[0]) | (taker == ranking[0]) | (lengths[taker] == 0), 0, jnp.maximum(margin, 0))
    moved = jax.random.randint(jax.random.fold_in(own, 4), (amount // 2,), 0, 1 << 20) % (margin + 1)
    lengths = lengths.at[source_of].add(-moved).at[taker].add(moved)
    labels = jnp.searchsorted(jnp.cumsum(lengths), jnp.arange(rows * top), side="right").astype(jnp.int32)
    grid = labels.reshape(top, rows).T
    grid = grid[jax.random.permutation(jax.random.fold_in(own, 1), rows)]
    rotation = jax.random.randint(jax.random.fold_in(own, 2), (rows, 1), 0, top)
    return jnp.take_along_axis(grid, (jnp.arange(top)[None, :] + rotation) % top, axis=1)


def portions_of(amount, total, most, slope, full):
    portions = [(1 << 20) // math.isqrt(rank ** slope) + 1 for rank in range(1, amount + 1)]
    largest = most if full else min(most, max(-(-total // amount), total * portions[0] // sum(portions)))
    least = 1 if total - largest >= amount - 1 else 0
    holding, surplus = [largest] + [least] * (amount - 1), total - largest - least * (amount - 1)
    while surplus > 0:
        movable = [i for i in range(1, amount) if holding[i] < largest] or [i for i in range(1, amount) if holding[i] < most]
        whole, remaining = sum([portions[i] for i in movable]), surplus
        for i in movable:
            addition = min(most - holding[i], max(1, remaining * portions[i] // whole), surplus)
            holding[i] = holding[i] + addition
            surplus = surplus - addition
    return np.array(holding)


def bell_draw(key, extent, deviation, reach, shards=(), kind=jnp.bfloat16):
    entries = deviation * jax.random.normal(key, extent, jnp.float32)
    if shards:
        entries = entries * steps_of(key, extent, shards, -0.22, 0.18)
    return jnp.clip(entries, -reach, reach).astype(kind)


def setup_inputs(seed: int = 0, part: int = 0) -> dict:
    key_list = jax.random.split(jax.random.key(seed), 7)
    part_keys = jax.random.split(jax.random.fold_in(key_list[6], part), 7)
    tokens = bell_draw(part_keys[0], (TOKENS, D), 1.0, 6.0, ((0, 32),))
    routes_keys = jax.random.split(jax.random.fold_in(part_keys[1], 1), TOKENS // TOK_DEV)
    routes_turns = jax.random.permutation(jax.random.fold_in(part_keys[1], 3), TOKENS // TOK_DEV)
    routes = jax.vmap(lambda own, number: routed_block(jax.random.fold_in(part_keys[1], 2), own, number, TOK_DEV, EXPERTS, TOPK, CAP, 2))(routes_keys, routes_turns).reshape((TOKENS, TOPK))
    route_weight = jnp.clip(0.25 + 0.75 * jax.random.uniform(part_keys[2], (TOKENS, TOPK), jnp.float32) ** steps_of(part_keys[2], (TOKENS, TOPK), ((0, 32),), -0.2, 0.2), 0.25, 1.0)
    gate_weight = bell_draw(key_list[3], (N_LOCAL, D, HID), D ** -0.5, 0.0625, ((0, 32),))
    up_weight = bell_draw(key_list[4], (N_LOCAL, D, HID), D ** -0.5, 0.0625, ((0, 32),))
    down_weight = bell_draw(key_list[5], (N_LOCAL, HID, D), FF ** -0.5, 0.125, ((0, 32),))
    return dict(tokens=tokens, routes=routes, route_weight=route_weight, gate_weight=gate_weight, up_weight=up_weight, down_weight=down_weight)


def reference(tokens, routes, route_weight, gate_weight, up_weight, down_weight):
    limit = N_LOCAL * CAP
    stacked = routes.reshape(-1)
    weights_flat = route_weight.reshape(-1)

    def one_expert(total, expert):
        start = (expert * SPLIT).astype(jnp.int32)
        gate_full = lax.dynamic_slice_in_dim(gate_weight, start, SPLIT, 0).transpose(1, 0, 2).reshape(D, FF)
        up_full = lax.dynamic_slice_in_dim(up_weight, start, SPLIT, 0).transpose(1, 0, 2).reshape(D, FF)
        down_full = lax.dynamic_slice_in_dim(down_weight, start, SPLIT, 0).reshape(FF, D)
        matched = stacked == expert
        positions = jnp.nonzero(matched, size=limit, fill_value=0)[0].astype(jnp.int32)
        valid = jnp.arange(limit) < jnp.sum(matched.astype(jnp.int32))
        row_index = positions // TOPK
        chosen = tokens[row_index]
        gate_part = jnp.dot(chosen, gate_full, preferred_element_type=jnp.float32)
        up_part = jnp.dot(chosen, up_full, preferred_element_type=jnp.float32)
        hidden = (jax.nn.silu(gate_part) * up_part).astype(jnp.bfloat16)
        result = jnp.dot(hidden, down_full, preferred_element_type=jnp.float32)
        scaling = jnp.where(valid, weights_flat[positions], jnp.float32(0.0))
        total = total.at[row_index].add(result * scaling[:, None])
        return total, None

    start_total = jnp.zeros((TOKENS, D), jnp.float32)
    total, _ = lax.scan(one_expert, start_total, jnp.arange(EXPERTS, dtype=jnp.int32))
    return total.astype(jnp.bfloat16)
```

```python
import jax
import jax.numpy as jnp
from jax import lax
from jax.sharding import PartitionSpec as P

SPLIT = 8
LANES = 128
GATHER_CHUNKS = 2
RETURN_CHUNKS = 2


def pieces(width, count):
    tiles = width // LANES
    edges = [tiles * i // count * LANES for i in range(count)] + [width]
    return list(zip(edges[:-1], edges[1:]))


def swap(members, mask):
    pairs = [(d, d ^ mask(d)) for d in range(members)]
    return lambda x: lax.ppermute(x, "local", pairs)


def body(tokens, routes, route_weight, gate_weight, up_weight, down_weight):
    members = lax.axis_size("local")
    experts = members // SPLIT
    rows_dev, features = tokens.shape
    rows = members * rows_dev
    fanout = routes.shape[1]

    expert_ids = jnp.arange(experts, dtype=jnp.int32)
    coef = sum(
        jnp.where(routes[:, k, None] == expert_ids, route_weight[:, k, None], 0.0)
        for k in range(fanout)
    )
    high = lax.reduce_precision(coef, 8, 7)
    middle = lax.reduce_precision(coef - high, 8, 7)
    low = coef - high - middle
    width = -(-3 * experts // LANES) * LANES
    terms = jnp.concatenate([high, middle, low], axis=1).astype(jnp.bfloat16)
    terms = jnp.pad(terms, ((0, 0), (0, width - 3 * experts)))

    outer = [swap(members, lambda d, e=e: e * SPLIT) for e in range(1, experts)]
    first = swap(members, lambda d: 4 if d & 1 else 2)
    second = swap(members, lambda d: 2 if d & 1 else 4)
    sibling = swap(members, lambda d: 1)

    def gather(x):
        x = jnp.concatenate([x] + [step(x) for step in outer], axis=0)
        for step in (first, second, sibling):
            x = jnp.concatenate([x, step(x)], axis=0)
        return x

    def give_back(x):
        for step in (sibling, second, first):
            kept, sent = jnp.split(x, 2, axis=0)
            x = kept + step(sent.astype(jnp.bfloat16)).astype(jnp.float32)
        blocks = jnp.split(x, experts, axis=0)
        total = blocks[0]
        for block, step in zip(blocks[1:], outer):
            total = total + step(block.astype(jnp.bfloat16)).astype(jnp.float32)
        return total.astype(jnp.bfloat16)

    gate_part = up_part = 0.0
    spans = pieces(features, GATHER_CHUNKS)
    for n, (lo, hi) in enumerate(spans):
        part = tokens[:, lo:hi]
        if n == len(spans) - 1:
            part = jnp.concatenate([part, terms], axis=1)
        lined = gather(part)
        if n == len(spans) - 1:
            arrived = lined[:, hi - lo :].astype(jnp.float32)
            lined = lined[:, : hi - lo]
        gate_part += jnp.dot(lined, gate_weight[0, lo:hi], preferred_element_type=jnp.float32)
        up_part += jnp.dot(lined, up_weight[0, lo:hi], preferred_element_type=jnp.float32)
    hidden = (jax.nn.silu(gate_part) * up_part).astype(jnp.bfloat16)

    mine = lax.axis_index("local") // SPLIT
    column = jnp.arange(width, dtype=jnp.int32)
    wanted = (column % experts == mine) & (column < 3 * experts)
    scale = jnp.sum(jnp.where(wanted, arrived, 0.0), axis=1, keepdims=True)

    results = []
    for lo, hi in pieces(features, RETURN_CHUNKS):
        result = jnp.dot(hidden, down_weight[0, :, lo:hi], preferred_element_type=jnp.float32)
        results.append(give_back(result * scale))
    return jnp.concatenate(results, axis=1)


def solution(mesh):
    return jax.shard_map(
        body,
        mesh=mesh,
        in_specs=(
            P(("parts", "local"), None),
            P(("parts", "local"), None),
            P(("parts", "local"), None),
            P("local", None, None),
            P("local", None, None),
            P("local", None, None),
        ),
        out_specs=P(("parts", "local"), None),
        check_vma=False,
    )
```

```python
import functools

import jax
import jax.numpy as jnp
from jax import lax
from jax.experimental import pallas as pl
from jax.experimental.pallas import tpu as pltpu
from jax.sharding import PartitionSpec as P

SPLIT = 8
LANES = 128
TILE = 512
MIB = 1 << 20
F32, BF16 = jnp.float32, jnp.bfloat16

VMEM = pl.BlockSpec(memory_space=pltpu.VMEM)
ANY = pl.BlockSpec(memory_space=pl.ANY)
HBM = pl.BlockSpec(memory_space=pltpu.HBM)
FREE = pl.CostEstimate(flops=0, bytes_accessed=0, transcendentals=0)


def swap(members, mask):
    pairs = [(d, d ^ mask(d)) for d in range(members)]
    return lambda x: lax.ppermute(x, "local", pairs)


def call(kernel, outs, operands, after=(), limit=8, scratch=()):
    count = len(operands)

    def run(*refs):
        kernel(*refs[:count], *refs[count + len(after) :])

    return pl.pallas_call(
        run,
        out_shape=[pltpu.VMEM(o.shape, o.dtype) for o in outs],
        in_specs=[VMEM] * count + [ANY] * len(after),
        out_specs=[VMEM] * len(outs),
        scratch_shapes=scratch,
        compiler_params=pltpu.CompilerParams(vmem_limit_bytes=limit * MIB),
        cost_estimate=FREE,
    )(*operands, *after)


def shape(rows, columns, dtype):
    return jax.ShapeDtypeStruct((rows, columns), dtype)


def pack_kernel(experts, tokens_hbm, routes_hbm, weight_hbm, out_ref, tokens_ref, routes_ref, weight_ref, sems):
    rows, features = tokens_ref.shape
    copies = [
        pltpu.make_async_copy(routes_hbm, routes_ref, sems.at[0]),
        pltpu.make_async_copy(weight_hbm, weight_ref, sems.at[1]),
        pltpu.make_async_copy(tokens_hbm, tokens_ref, sems.at[2]),
    ]
    for copy in copies:
        copy.start()
    for copy in copies:
        copy.wait()
    out_ref[:, :features] = tokens_ref[...]
    width = out_ref.shape[1] - features
    column = lax.broadcasted_iota(jnp.int32, (rows, width), 1)
    square = (rows, rows)
    own = lax.broadcasted_iota(jnp.int32, square, 0) == lax.broadcasted_iota(jnp.int32, square, 1)
    coef = jnp.zeros((rows, width), F32)
    for k in range(routes_ref.shape[0]):
        route = jnp.sum(jnp.where(own, routes_ref[k : k + 1, :], 0), axis=1, keepdims=True)
        weight = jnp.sum(jnp.where(own, weight_ref[k : k + 1, :], 0.0), axis=1, keepdims=True)
        coef += jnp.where(lax.rem(column, experts) == route, weight, 0.0)
    high = coef.astype(BF16).astype(F32)
    middle = (coef - high).astype(BF16).astype(F32)
    low = coef - high - middle
    terms = jnp.where(column < experts, high, jnp.where(column < 2 * experts, middle, low))
    out_ref[:, features:] = jnp.where(column < 3 * experts, terms, 0.0).astype(BF16)


def stack_kernel(a_ref, b_ref, out_ref):
    out_ref[...] = jnp.concatenate([a_ref[...], b_ref[...]], axis=0)


def gate_kernel(pieces, experts, mine_ref, *refs):
    x_refs, (gate_ref, up_ref), (hidden_ref, scale_ref) = refs[:pieces], refs[pieces : pieces + 2], refs[-2:]
    features = gate_ref.shape[0]
    gate = up = jnp.zeros(hidden_ref.shape, F32)
    for lo in range(0, features, TILE):
        x = jnp.concatenate([r[:, lo : lo + TILE] for r in x_refs], axis=0)
        gate += jnp.dot(x, gate_ref[lo : lo + TILE, :], preferred_element_type=F32)
        up += jnp.dot(x, up_ref[lo : lo + TILE, :], preferred_element_type=F32)
    hidden_ref[...] = (jax.nn.silu(gate) * up).astype(BF16)
    terms = jnp.concatenate([r[:, features:] for r in x_refs], axis=0).astype(F32)
    column = lax.broadcasted_iota(jnp.int32, terms.shape, 1)
    wanted = (lax.rem(column, experts) == mine_ref[0]) & (column < 3 * experts)
    scale = jnp.sum(jnp.where(wanted, terms, 0.0), axis=1, keepdims=True)
    scale_ref[...] = jnp.broadcast_to(scale, scale_ref.shape)


def down_kernel(start, hidden_ref, scale_ref, down_ref, kept_ref, sent_ref):
    half, features = kept_ref.shape
    hidden = hidden_ref[start : start + 2 * half, :]
    scale = scale_ref[start : start + 2 * half, :1]
    for lo in range(0, features, TILE):
        tile = slice(lo, lo + TILE)
        out = jnp.dot(hidden, down_ref[:, tile], preferred_element_type=F32) * scale
        kept_ref[:, tile] = out[:half]
        sent_ref[:, tile] = out[half:].astype(BF16)


def add_kernel(kept_ref, got_ref, next_ref, sent_ref):
    half = next_ref.shape[0]
    total = kept_ref[...] + got_ref[...].astype(F32)
    next_ref[...] = total[:half]
    sent_ref[...] = total[half:].astype(BF16)


def close_kernel(kept_ref, *refs):
    total = kept_ref[...]
    for got_ref in refs[:-1]:
        total += got_ref[...].astype(F32)
    refs[-1][...] = total.astype(BF16)


def load_kernel(*refs):
    count = (len(refs) - 1) // 2
    copies = [
        pltpu.make_async_copy(src, dst, refs[-1].at[i])
        for i, (src, dst) in enumerate(zip(refs[:count], refs[count:-1]))
    ]
    for copy in copies:
        copy.start()
    for copy in copies:
        copy.wait()


def load(arrays, after):
    count = len(arrays)

    def run(*refs):
        load_kernel(*refs[:count], *refs[count + len(after) :])

    return pl.pallas_call(
        run,
        out_shape=[pltpu.VMEM(a.shape, a.dtype) for a in arrays],
        in_specs=[HBM] * count + [ANY] * len(after),
        out_specs=[VMEM] * count,
        scratch_shapes=[pltpu.SemaphoreType.DMA((count,))],
        compiler_params=pltpu.CompilerParams(vmem_limit_bytes=MIB),
        cost_estimate=FREE,
    )(*[pltpu.with_memory_space_constraint(a, pltpu.HBM) for a in arrays], *after)


def body(tokens, routes, route_weight, gate_weight, up_weight, down_weight):
    members = lax.axis_size("local")
    experts = members // SPLIT
    rows, features = tokens.shape
    hid = gate_weight.shape[2]

    width = -(-3 * experts // LANES) * LANES
    full = features + width
    sources = [tokens, routes.T, route_weight.T]
    payload = pl.pallas_call(
        functools.partial(pack_kernel, experts),
        out_shape=pltpu.VMEM((rows, full), BF16),
        in_specs=[HBM] * 3,
        out_specs=VMEM,
        scratch_shapes=[pltpu.VMEM(x.shape, x.dtype) for x in sources] + [pltpu.SemaphoreType.DMA((3,))],
        compiler_params=pltpu.CompilerParams(vmem_limit_bytes=MIB),
        cost_estimate=FREE,
    )(*[pltpu.with_memory_space_constraint(x, pltpu.HBM) for x in sources])

    outer = {e: swap(members, lambda d, e=e: (e & -e) * SPLIT) for e in range(1, experts)}
    first = swap(members, lambda d: 4 if d & 1 else 2)
    second = swap(members, lambda d: 2 if d & 1 else 4)
    sibling = swap(members, lambda d: 1)
    order = list(range(experts))

    blocks = {0: payload}
    for e in order[1:]:
        blocks[e] = outer[e](blocks[e & (e - 1)])
    pieces, last = {}, ()
    for n, e in enumerate(order):
        if n > 1:
            blocks[e], _ = lax.optimization_barrier((blocks[e], pieces[order[0]][0]))
        (pair,) = call(
            stack_kernel, [shape(2 * rows, full, BF16)], [blocks[e], first(blocks[e])], last
        )
        far = second(pair)
        pieces[e] = [pair, far, sibling(pair), sibling(far)]
        last = (pair, pieces[order[0]][1]) if n else (pair,)

    gate, up, down = load([gate_weight[0], up_weight[0], down_weight[0]], last)
    mine = (lax.axis_index("local") // SPLIT).astype(jnp.int32)[None]
    hidden_of, last = {}, ()
    for at in range(0, experts, 2):
        batch = order[at : at + 2]
        xs = [p for e in batch for p in pieces[e]]
        height = sum(x.shape[0] for x in xs)
        hidden, scale = pl.pallas_call(
            functools.partial(gate_kernel, len(xs), experts),
            out_shape=[pltpu.VMEM((height, hid), BF16), pltpu.VMEM((height, LANES), F32)],
            in_specs=[pl.BlockSpec(memory_space=pltpu.SMEM)] + [VMEM] * (len(xs) + 2) + [ANY] * len(last),
            out_specs=[VMEM, VMEM],
            compiler_params=pltpu.CompilerParams(vmem_limit_bytes=8 * MIB),
            cost_estimate=FREE,
        )(mine, *xs, gate, up, *last)
        last = (hidden,)
        for n, e in enumerate(batch):
            hidden_of[e] = (n * height // len(batch), hidden, scale)

    def descend(e, after):
        start, hidden, scale = hidden_of[e]
        half = SPLIT * rows // 2
        return call(
            functools.partial(down_kernel, start),
            [shape(half, features, F32), shape(half, features, BF16)],
            [hidden, scale, down],
            after,
        )

    def add(kept, got, after):
        half = kept.shape[0] // 2
        return call(add_kernel, [shape(half, features, F32), shape(half, features, BF16)], [kept, got], after)

    def close(kept, gots, after):
        return call(close_kernel, [shape(rows, features, BF16)], [kept, *gots], after)[0]

    back = order[::-1]
    state, last, home = {}, (), {e: [] for e in order}
    lag = (0, 1, 3, 4)
    for slot in range(len(back) + lag[-1]):
        for stage in range(4):
            n = slot - lag[stage]
            if not 0 <= n < len(back):
                continue
            e = back[n]
            if stage == 0:
                kept, sent = descend(e, last)
                state[e] = (kept, sibling(sent))
            elif stage == 1:
                kept, sent = add(*state[e], last)
                state[e] = (kept, second(sent))
            elif stage == 2:
                kept, sent = add(*state[e], last)
                state[e] = (kept, first(sent))
            else:
                sent = close(state[e][0], [state[e][1], *home[e]], last)
                if not e:
                    return sent
                home[e & (e - 1)].append(outer[e](sent))
            last = (sent,)


def solution(mesh):
    return jax.shard_map(
        body,
        mesh=mesh,
        in_specs=(
            P(("parts", "local"), None),
            P(("parts", "local"), None),
            P(("parts", "local"), None),
            P("local", None, None),
            P("local", None, None),
            P("local", None, None),
        ),
        out_specs=P(("parts", "local"), None),
        check_vma=False,
    )
```

```python
import functools

import jax
import jax.numpy as jnp
from jax import lax
from jax.experimental import pallas as pl
from jax.experimental.pallas import tpu as pltpu
from jax.sharding import PartitionSpec as P

SPLIT = 8
LANES = 128
TILE = 512
MIB = 1 << 20
F32, BF16 = jnp.float32, jnp.bfloat16

VMEM = pl.BlockSpec(memory_space=pltpu.VMEM)
ANY = pl.BlockSpec(memory_space=pl.ANY)
HBM = pl.BlockSpec(memory_space=pltpu.HBM)


def cost(us):
    return pl.CostEstimate(flops=0, bytes_accessed=int(us * 3.6e6), transcendentals=0)


def swap(members, mask):
    pairs = [(d, d ^ mask(d)) for d in range(members)]
    return lambda x: lax.ppermute(x, "local", pairs)


def call(kernel, outs, operands, after=(), limit=8):
    count = len(operands)

    def run(*refs):
        kernel(*refs[:count], *refs[count + len(after) :])

    return pl.pallas_call(
        run,
        out_shape=[pltpu.VMEM(o.shape, o.dtype) for o in outs],
        in_specs=[VMEM] * count + [ANY] * len(after),
        out_specs=[VMEM] * len(outs),
        compiler_params=pltpu.CompilerParams(vmem_limit_bytes=limit * MIB),
        cost_estimate=cost(0),
    )(*operands, *after)


def shape(rows, columns, dtype):
    return jax.ShapeDtypeStruct((rows, columns), dtype)


def pack_kernel(experts, tokens_hbm, routes_hbm, weight_hbm, out_ref, tokens_ref, routes_ref, weight_ref, sems):
    rows, features = tokens_ref.shape
    copies = [
        pltpu.make_async_copy(routes_hbm, routes_ref, sems.at[0]),
        pltpu.make_async_copy(weight_hbm, weight_ref, sems.at[1]),
        pltpu.make_async_copy(tokens_hbm, tokens_ref, sems.at[2]),
    ]
    for copy in copies:
        copy.start()
    for copy in copies:
        copy.wait()
    out_ref[:, :features] = tokens_ref[...]
    width = out_ref.shape[1] - features
    column = lax.broadcasted_iota(jnp.int32, (rows, width), 1)
    square = (rows, rows)
    own = lax.broadcasted_iota(jnp.int32, square, 0) == lax.broadcasted_iota(jnp.int32, square, 1)
    coef = jnp.zeros((rows, width), F32)
    for k in range(routes_ref.shape[0]):
        route = jnp.sum(jnp.where(own, routes_ref[k : k + 1, :], 0), axis=1, keepdims=True)
        weight = jnp.sum(jnp.where(own, weight_ref[k : k + 1, :], 0.0), axis=1, keepdims=True)
        coef += jnp.where(lax.rem(column, experts) == route, weight, 0.0)
    high = coef.astype(BF16).astype(F32)
    middle = (coef - high).astype(BF16).astype(F32)
    low = coef - high - middle
    terms = jnp.where(column < experts, high, jnp.where(column < 2 * experts, middle, low))
    out_ref[:, features:] = jnp.where(column < 3 * experts, terms, 0.0).astype(BF16)


def stack_kernel(*refs):
    refs[-1][...] = jnp.concatenate([r[...] for r in refs[:-1]], axis=0)


def gate_kernel(pieces, experts, mine_ref, *refs):
    x_refs, (gate_ref, up_ref), (hidden_ref, scale_ref) = refs[:pieces], refs[pieces : pieces + 2], refs[-2:]
    features = gate_ref.shape[0]
    gate = up = jnp.zeros(hidden_ref.shape, F32)
    for lo in range(0, features, TILE):
        x = jnp.concatenate([r[:, lo : lo + TILE] for r in x_refs], axis=0)
        gate += jnp.dot(x, gate_ref[lo : lo + TILE, :], preferred_element_type=F32)
        up += jnp.dot(x, up_ref[lo : lo + TILE, :], preferred_element_type=F32)
    hidden_ref[...] = (jax.nn.silu(gate) * up).astype(BF16)
    terms = jnp.concatenate([r[:, features:] for r in x_refs], axis=0).astype(F32)
    column = lax.broadcasted_iota(jnp.int32, terms.shape, 1)
    wanted = (lax.rem(column, experts) == mine_ref[0]) & (column < 3 * experts)
    scale = jnp.sum(jnp.where(wanted, terms, 0.0), axis=1, keepdims=True)
    scale_ref[...] = jnp.broadcast_to(scale, scale_ref.shape)


def down_kernel(start, hidden_ref, scale_ref, down_ref, kept_ref, sent_ref):
    half, features = kept_ref.shape
    hidden = hidden_ref[start : start + 2 * half, :]
    scale = scale_ref[start : start + 2 * half, :1]
    for lo in range(0, features, TILE):
        tile = slice(lo, lo + TILE)
        out = jnp.dot(hidden, down_ref[:, tile], preferred_element_type=F32) * scale
        kept_ref[:, tile] = out[:half]
        sent_ref[:, tile] = out[half:].astype(BF16)


def add_kernel(kept_ref, got_ref, next_ref, sent_ref):
    half = next_ref.shape[0]
    total = kept_ref[...] + got_ref[...].astype(F32)
    next_ref[...] = total[:half]
    sent_ref[...] = total[half:].astype(BF16)


def close_kernel(kept_ref, *refs):
    total = kept_ref[...]
    for got_ref in refs[:-1]:
        total += got_ref[...].astype(F32)
    refs[-1][...] = total.astype(BF16)


def load(arrays, after):
    count, parts = len(arrays), 2

    def run(*refs):
        outs, sems = refs[count + len(after) : -1], refs[-1]
        copies = []
        for i in range(count):
            height = arrays[i].shape[0] // parts
            for n in range(parts):
                rows = pl.ds(n * height, height)
                copies.append(pltpu.make_async_copy(refs[i].at[rows], outs[i].at[rows], sems.at[i, n]))
        for copy in copies:
            copy.start()
        for copy in copies:
            copy.wait()

    return pl.pallas_call(
        run,
        out_shape=[pltpu.VMEM(a.shape, a.dtype) for a in arrays],
        in_specs=[HBM] * count + [ANY] * len(after),
        out_specs=[VMEM] * count,
        scratch_shapes=[pltpu.SemaphoreType.DMA((count, parts))],
        compiler_params=pltpu.CompilerParams(vmem_limit_bytes=MIB),
        cost_estimate=cost(4),
    )(*[pltpu.with_memory_space_constraint(a, pltpu.HBM) for a in arrays], *after)


def plan(experts):
    near, far = range(experts // 2), range(experts // 2, experts)
    steps = [("fetch", e) for e in sorted(range(1, experts), key=lambda e: (bin(e).count("1"), -e))]
    steps += [("behind", far[0]), ("stack", 0), ("behind", far[-1])] + [("stack", e) for e in range(1, experts)]
    steps += [("load",)]
    for e in near[::2]:
        steps += [("gate", (e, e + 1)), ("down", e + 1), ("down", e)]
    steps += [("hold", e, near[-2]) for e in far]
    steps += [("gate", (e, e + 1)) for e in far[::2]] + [("down", e) for e in far[::-1]]
    back = range(experts)[::-1]
    for slot in range(experts + 3):
        for step, lag in (("add1", 0), ("add2", 2), ("close", 3)):
            if 0 <= slot - lag < experts:
                steps.append((step, back[slot - lag]))
    return steps


def body(tokens, routes, route_weight, gate_weight, up_weight, down_weight):
    members = lax.axis_size("local")
    experts = members // SPLIT
    rows, features = tokens.shape
    hid = gate_weight.shape[2]

    width = -(-3 * experts // LANES) * LANES
    full = features + width
    sources = [tokens, routes.T, route_weight.T]
    payload = pl.pallas_call(
        functools.partial(pack_kernel, experts),
        out_shape=pltpu.VMEM((rows, full), BF16),
        in_specs=[HBM] * 3,
        out_specs=VMEM,
        scratch_shapes=[pltpu.VMEM(x.shape, x.dtype) for x in sources] + [pltpu.SemaphoreType.DMA((3,))],
        compiler_params=pltpu.CompilerParams(vmem_limit_bytes=MIB),
        cost_estimate=cost(0),
    )(*[pltpu.with_memory_space_constraint(x, pltpu.HBM) for x in sources])

    outer = {e: swap(members, lambda d, e=e: (e & -e) * SPLIT) for e in range(1, experts)}
    first = swap(members, lambda d: 4 if d & 1 else 2)
    second = swap(members, lambda d: 2 if d & 1 else 4)
    sibling = swap(members, lambda d: 1)
    mine = (lax.axis_index("local") // SPLIT).astype(jnp.int32)[None]
    weights = [gate_weight[0], up_weight[0], down_weight[0]]
    height = SPLIT * rows
    blocks, pairs, fars, nears, downs = {0: payload}, {}, {}, {}, {}
    hidden_of, state, home = {}, {}, {e: [] for e in range(experts)}
    last = (payload,)
    for step, *at in plan(experts):
        e = at[0] if at else None
        if step == "fetch":
            blocks[e] = outer[e](blocks[e & (e - 1)])
            continue
        if step == "behind":
            last = (*last, blocks[e])
            continue
        if step == "hold":
            fars[e], _ = lax.optimization_barrier((fars[e], downs[at[1]]))
            continue
        if step == "stack":
            (out,) = call(stack_kernel, [shape(2 * rows, full, BF16)], [blocks[e], first(blocks[e])], last)
            pairs[e], fars[e], nears[e] = out, second(out), sibling(out)
        elif step == "load":
            weights = load(weights, last)
            out = weights[0]
        elif step == "gate":
            xs = [x for g in e for x in (pairs[g], fars[g], nears[g], sibling(fars[g]))]
            out, scale = pl.pallas_call(
                functools.partial(gate_kernel, len(xs), experts),
                out_shape=[pltpu.VMEM((2 * height, hid), BF16), pltpu.VMEM((2 * height, LANES), F32)],
                in_specs=[pl.BlockSpec(memory_space=pltpu.SMEM)] + [VMEM] * (len(xs) + 2) + [ANY] * len(last),
                out_specs=[VMEM, VMEM],
                compiler_params=pltpu.CompilerParams(vmem_limit_bytes=8 * MIB),
                cost_estimate=cost(0),
            )(mine, *xs, weights[0], weights[1], *last)
            for n, g in enumerate(e):
                hidden_of[g] = (n * height, out, scale)
        elif step == "down":
            begin, hidden, scale = hidden_of[e]
            half = height // 2
            kept, out = call(
                functools.partial(down_kernel, begin),
                [shape(half, features, F32), shape(half, features, BF16)],
                [hidden, scale, weights[2]],
                last,
            )
            downs[e] = out
            state[e] = (kept, sibling(out))
        elif step in ("add1", "add2"):
            kept, got = state[e]
            half = kept.shape[0] // 2
            kept, out = call(
                add_kernel, [shape(half, features, F32), shape(half, features, BF16)], [kept, got], last
            )
            state[e] = (kept, (second if step == "add1" else first)(out))
        else:
            (out,) = call(close_kernel, [shape(rows, features, BF16)], [*state[e], *home[e]], last)
            if not e:
                return out
            home[e & (e - 1)].append(outer[e](out))
        last = (out,)


def solution(mesh):
    return jax.shard_map(
        body,
        mesh=mesh,
        in_specs=(
            P(("parts", "local"), None),
            P(("parts", "local"), None),
            P(("parts", "local"), None),
            P("local", None, None),
            P("local", None, None),
            P("local", None, None),
        ),
        out_specs=P(("parts", "local"), None),
        check_vma=False,
    )
```

```python
import functools

import jax
import jax.numpy as jnp
from jax import lax
from jax.experimental import pallas as pl
from jax.experimental.pallas import tpu as pltpu
from jax.sharding import PartitionSpec as P

SPLIT = 8
LANES = 128
TILE = 512
MIB = 1 << 20
F32, BF16 = jnp.float32, jnp.bfloat16

VMEM = pl.BlockSpec(memory_space=pltpu.VMEM)
ANY = pl.BlockSpec(memory_space=pl.ANY)
HBM = pl.BlockSpec(memory_space=pltpu.HBM)


def cost(us):
    return pl.CostEstimate(flops=0, bytes_accessed=int(us * 3.6e6), transcendentals=0)


def swap(members, mask):
    pairs = [(d, d ^ mask(d)) for d in range(members)]
    return lambda x: lax.ppermute(x, "local", pairs)


def call(kernel, outs, operands, after=(), limit=8):
    count = len(operands)

    def run(*refs):
        kernel(*refs[:count], *refs[count + len(after) :])

    return pl.pallas_call(
        run,
        out_shape=[pltpu.VMEM(o.shape, o.dtype) for o in outs],
        in_specs=[VMEM] * count + [ANY] * len(after),
        out_specs=[VMEM] * len(outs),
        compiler_params=pltpu.CompilerParams(vmem_limit_bytes=limit * MIB),
        cost_estimate=cost(0),
    )(*operands, *after)


def shape(rows, columns, dtype):
    return jax.ShapeDtypeStruct((rows, columns), dtype)


def pack_kernel(experts, tokens_hbm, routes_hbm, weight_hbm, out_ref, tokens_ref, routes_ref, weight_ref, sems):
    rows, features = tokens_ref.shape
    copies = [
        pltpu.make_async_copy(routes_hbm, routes_ref, sems.at[0]),
        pltpu.make_async_copy(weight_hbm, weight_ref, sems.at[1]),
        pltpu.make_async_copy(tokens_hbm, tokens_ref, sems.at[2]),
    ]
    for copy in copies:
        copy.start()
    for copy in copies:
        copy.wait()
    out_ref[:, :features] = tokens_ref[...]
    width = out_ref.shape[1] - features
    column = lax.broadcasted_iota(jnp.int32, (rows, width), 1)
    square = (rows, rows)
    own = lax.broadcasted_iota(jnp.int32, square, 0) == lax.broadcasted_iota(jnp.int32, square, 1)
    coef = jnp.zeros((rows, width), F32)
    for k in range(routes_ref.shape[0]):
        route = jnp.sum(jnp.where(own, routes_ref[k : k + 1, :], 0), axis=1, keepdims=True)
        weight = jnp.sum(jnp.where(own, weight_ref[k : k + 1, :], 0.0), axis=1, keepdims=True)
        coef += jnp.where(lax.rem(column, experts) == route, weight, 0.0)
    high = coef.astype(BF16).astype(F32)
    middle = (coef - high).astype(BF16).astype(F32)
    low = coef - high - middle
    terms = jnp.where(column < experts, high, jnp.where(column < 2 * experts, middle, low))
    out_ref[:, features:] = jnp.where(column < 3 * experts, terms, 0.0).astype(BF16)


def stack_kernel(*refs):
    refs[-1][...] = jnp.concatenate([r[...] for r in refs[:-1]], axis=0)


def gate_kernel(pieces, experts, mine_ref, *refs):
    x_refs, (gate_ref, up_ref), (hidden_ref, scale_ref) = refs[:pieces], refs[pieces : pieces + 2], refs[-2:]
    features = gate_ref.shape[0]
    gate = up = jnp.zeros(hidden_ref.shape, F32)
    for lo in range(0, features, TILE):
        x = jnp.concatenate([r[:, lo : lo + TILE] for r in x_refs], axis=0)
        gate += jnp.dot(x, gate_ref[lo : lo + TILE, :], preferred_element_type=F32)
        up += jnp.dot(x, up_ref[lo : lo + TILE, :], preferred_element_type=F32)
    hidden_ref[...] = (jax.nn.silu(gate) * up).astype(BF16)
    terms = jnp.concatenate([r[:, features:] for r in x_refs], axis=0).astype(F32)
    column = lax.broadcasted_iota(jnp.int32, terms.shape, 1)
    wanted = (lax.rem(column, experts) == mine_ref[0]) & (column < 3 * experts)
    scale = jnp.sum(jnp.where(wanted, terms, 0.0), axis=1, keepdims=True)
    scale_ref[...] = jnp.broadcast_to(scale, scale_ref.shape)


def down_kernel(hidden_ref, scale_ref, down_ref, *refs):
    half, features = refs[0].shape
    for lo in range(0, features, TILE):
        tile = slice(lo, lo + TILE)
        out = jnp.dot(hidden_ref[...], down_ref[:, tile], preferred_element_type=F32) * scale_ref[:, :1]
        for n in range(2):
            begin = 2 * n * half
            refs[2 * n][:, tile] = out[begin : begin + half]
            refs[2 * n + 1][:, tile] = out[begin + half : begin + 2 * half].astype(BF16)


def add_kernel(kept_ref, got_ref, next_ref, sent_ref):
    half = next_ref.shape[0]
    total = kept_ref[...] + got_ref[...].astype(F32)
    next_ref[...] = total[:half]
    sent_ref[...] = total[half:].astype(BF16)


def close_kernel(kept_ref, *refs):
    total = kept_ref[...]
    for got_ref in refs[:-1]:
        total += got_ref[...].astype(F32)
    refs[-1][...] = total.astype(BF16)


def load(arrays, after):
    count, parts = len(arrays), 8

    def run(*refs):
        outs, sems = refs[count + len(after) : -1], refs[-1]
        copies = []
        for i in range(count):
            height = arrays[i].shape[0] // parts
            for n in range(parts):
                rows = pl.ds(n * height, height)
                copies.append(pltpu.make_async_copy(refs[i].at[rows], outs[i].at[rows], sems.at[i, n]))
        for copy in copies:
            copy.start()
        for copy in copies:
            copy.wait()

    return pl.pallas_call(
        run,
        out_shape=[pltpu.VMEM(a.shape, a.dtype) for a in arrays],
        in_specs=[HBM] * count + [ANY] * len(after),
        out_specs=[VMEM] * count,
        scratch_shapes=[pltpu.SemaphoreType.DMA((count, parts))],
        compiler_params=pltpu.CompilerParams(vmem_limit_bytes=MIB),
        cost_estimate=cost(4),
    )(*[pltpu.with_memory_space_constraint(a, pltpu.HBM) for a in arrays], *after)


def plan(experts):
    near, far = range(experts // 2), range(experts // 2, experts)
    steps = [("fetch", e) for e in sorted(range(1, experts), key=lambda e: (bin(e).count("1"), -e))]
    steps += [("behind", far[0]), ("stack", 0), ("behind", far[-1])] + [("stack", e) for e in range(1, experts)]
    steps += [("load",)]
    steps += [("gate", (e, e + 1)) for e in near[::2]]
    steps += [("hold", e, (near[-2], near[-1])) for e in far]
    steps += [("down", (e, e + 1)) for e in near[::2]]
    steps += [("gate", (e, e + 1)) for e in far[::2]]
    steps += [("down", (e, e + 1)) for e in far[::2][::-1]]
    back = range(experts)[::-1]
    for slot in range(experts + 3):
        for step, lag in (("add1", 0), ("add2", 2), ("close", 3)):
            if 0 <= slot - lag < experts:
                steps.append((step, back[slot - lag]))
    return steps


def body(tokens, routes, route_weight, gate_weight, up_weight, down_weight):
    members = lax.axis_size("local")
    experts = members // SPLIT
    rows, features = tokens.shape
    hid = gate_weight.shape[2]

    width = -(-3 * experts // LANES) * LANES
    full = features + width
    sources = [tokens, routes.T, route_weight.T]
    payload = pl.pallas_call(
        functools.partial(pack_kernel, experts),
        out_shape=pltpu.VMEM((rows, full), BF16),
        in_specs=[HBM] * 3,
        out_specs=VMEM,
        scratch_shapes=[pltpu.VMEM(x.shape, x.dtype) for x in sources] + [pltpu.SemaphoreType.DMA((3,))],
        compiler_params=pltpu.CompilerParams(vmem_limit_bytes=MIB),
        cost_estimate=cost(0),
    )(*[pltpu.with_memory_space_constraint(x, pltpu.HBM) for x in sources])

    outer = {e: swap(members, lambda d, e=e: (e & -e) * SPLIT) for e in range(1, experts)}
    first = swap(members, lambda d: 4 if d & 1 else 2)
    second = swap(members, lambda d: 2 if d & 1 else 4)
    sibling = swap(members, lambda d: 1)
    mine = (lax.axis_index("local") // SPLIT).astype(jnp.int32)[None]
    weights = [gate_weight[0], up_weight[0], down_weight[0]]
    height = SPLIT * rows
    blocks, pairs, fars, nears = {0: payload}, {}, {}, {}
    hidden_of, state, home = {}, {}, {e: [] for e in range(experts)}
    last = (payload,)
    for step, *at in plan(experts):
        e = at[0] if at else None
        if step == "fetch":
            blocks[e] = outer[e](blocks[e & (e - 1)])
            continue
        if step == "behind":
            last = (*last, blocks[e])
            continue
        if step == "hold":
            fars[e], _ = lax.optimization_barrier((fars[e], hidden_of[at[1]][0]))
            continue
        if step == "stack":
            (out,) = call(stack_kernel, [shape(2 * rows, full, BF16)], [blocks[e], first(blocks[e])], last)
            pairs[e], fars[e], nears[e] = out, second(out), sibling(out)
        elif step == "load":
            weights = load(weights, last)
            out = weights[0]
        elif step == "gate":
            xs = [x for g in e for x in (pairs[g], fars[g], nears[g], sibling(fars[g]))]
            out, scale = pl.pallas_call(
                functools.partial(gate_kernel, len(xs), experts),
                out_shape=[pltpu.VMEM((2 * height, hid), BF16), pltpu.VMEM((2 * height, LANES), F32)],
                in_specs=[pl.BlockSpec(memory_space=pltpu.SMEM)] + [VMEM] * (len(xs) + 2) + [ANY] * len(last),
                out_specs=[VMEM, VMEM],
                compiler_params=pltpu.CompilerParams(vmem_limit_bytes=8 * MIB),
                cost_estimate=cost(0),
            )(mine, *xs, weights[0], weights[1], *last)
            hidden_of[e] = (out, scale)
        elif step == "down":
            half = height // 2
            made = call(
                down_kernel,
                [shape(half, features, t) for t in (F32, BF16, F32, BF16)],
                [*hidden_of[e], weights[2]],
                last,
            )
            out = made[-1]
            state[e[1]], state[e[0]] = (made[2], sibling(out)), (made[0], sibling(made[1]))
        elif step in ("add1", "add2"):
            kept, got = state[e]
            half = kept.shape[0] // 2
            kept, out = call(
                add_kernel, [shape(half, features, F32), shape(half, features, BF16)], [kept, got], last
            )
            state[e] = (kept, (second if step == "add1" else first)(out))
        else:
            (out,) = call(close_kernel, [shape(rows, features, BF16)], [*state[e], *home[e]], last)
            if not e:
                return out
            home[e & (e - 1)].append(outer[e](out))
        last = (out,)


def solution(mesh):
    return jax.shard_map(
        body,
        mesh=mesh,
        in_specs=(
            P(("parts", "local"), None),
            P(("parts", "local"), None),
            P(("parts", "local"), None),
            P("local", None, None),
            P("local", None, None),
            P("local", None, None),
        ),
        out_specs=P(("parts", "local"), None),
        check_vma=False,
    )
```

```python
import functools

import jax
import jax.numpy as jnp
from jax import lax
from jax.experimental import pallas as pl
from jax.experimental.pallas import tpu as pltpu
from jax.sharding import PartitionSpec as P

SPLIT = 8
LANES = 128
TILE = 512
MIB = 1 << 20
F32, BF16 = jnp.float32, jnp.bfloat16

VMEM = pl.BlockSpec(memory_space=pltpu.VMEM)
ANY = pl.BlockSpec(memory_space=pl.ANY)
HBM = pl.BlockSpec(memory_space=pltpu.HBM)


def cost(us):
    return pl.CostEstimate(flops=0, bytes_accessed=int(us * 3.6e6), transcendentals=0)


def swap(members, mask):
    pairs = [(d, d ^ mask(d)) for d in range(members)]
    return lambda x: lax.ppermute(x, "local", pairs)


def call(kernel, outs, operands, after=(), limit=8):
    count = len(operands)

    def run(*refs):
        kernel(*refs[:count], *refs[count + len(after) :])

    return pl.pallas_call(
        run,
        out_shape=[pltpu.VMEM(o.shape, o.dtype) for o in outs],
        in_specs=[VMEM] * count + [ANY] * len(after),
        out_specs=[VMEM] * len(outs),
        compiler_params=pltpu.CompilerParams(vmem_limit_bytes=limit * MIB),
        cost_estimate=cost(0),
    )(*operands, *after)


def shape(rows, columns, dtype):
    return jax.ShapeDtypeStruct((rows, columns), dtype)


def pack_kernel(experts, tokens_hbm, routes_hbm, weight_hbm, out_ref, tokens_ref, routes_ref, weight_ref, sems):
    rows, features = tokens_ref.shape
    copies = [
        pltpu.make_async_copy(routes_hbm, routes_ref, sems.at[0]),
        pltpu.make_async_copy(weight_hbm, weight_ref, sems.at[1]),
        pltpu.make_async_copy(tokens_hbm, tokens_ref, sems.at[2]),
    ]
    for copy in copies:
        copy.start()
    for copy in copies:
        copy.wait()
    out_ref[:, :features] = tokens_ref[...]
    width = out_ref.shape[1] - features
    column = lax.broadcasted_iota(jnp.int32, (rows, width), 1)
    square = (rows, rows)
    own = lax.broadcasted_iota(jnp.int32, square, 0) == lax.broadcasted_iota(jnp.int32, square, 1)
    coef = jnp.zeros((rows, width), F32)
    for k in range(routes_ref.shape[0]):
        route = jnp.sum(jnp.where(own, routes_ref[k : k + 1, :], 0), axis=1, keepdims=True)
        weight = jnp.sum(jnp.where(own, weight_ref[k : k + 1, :], 0.0), axis=1, keepdims=True)
        coef += jnp.where(lax.rem(column, experts) == route, weight, 0.0)
    high = coef.astype(BF16).astype(F32)
    middle = (coef - high).astype(BF16).astype(F32)
    low = coef - high - middle
    terms = jnp.where(column < experts, high, jnp.where(column < 2 * experts, middle, low))
    out_ref[:, features:] = jnp.where(column < 3 * experts, terms, 0.0).astype(BF16)


def stack_kernel(*refs):
    refs[-1][...] = jnp.concatenate([r[...] for r in refs[:-1]], axis=0)


def gate_kernel(pieces, experts, mine_ref, *refs):
    x_refs, (gate_ref, up_ref), (hidden_ref, scale_ref) = refs[:pieces], refs[pieces : pieces + 2], refs[-2:]
    features = gate_ref.shape[0]
    gate = up = jnp.zeros(hidden_ref.shape, F32)
    for lo in range(0, features, TILE):
        x = jnp.concatenate([r[:, lo : lo + TILE] for r in x_refs], axis=0)
        gate += jnp.dot(x, gate_ref[lo : lo + TILE, :], preferred_element_type=F32)
        up += jnp.dot(x, up_ref[lo : lo + TILE, :], preferred_element_type=F32)
    hidden_ref[...] = (jax.nn.silu(gate) * up).astype(BF16)
    terms = jnp.concatenate([r[:, features:] for r in x_refs], axis=0).astype(F32)
    column = lax.broadcasted_iota(jnp.int32, terms.shape, 1)
    wanted = (lax.rem(column, experts) == mine_ref[0]) & (column < 3 * experts)
    scale = jnp.sum(jnp.where(wanted, terms, 0.0), axis=1, keepdims=True)
    scale_ref[...] = jnp.broadcast_to(scale, scale_ref.shape)


def down_kernel(hidden_ref, scale_ref, down_ref, *refs):
    half, features = refs[0].shape
    for lo in range(0, features, TILE):
        tile = slice(lo, lo + TILE)
        out = jnp.dot(hidden_ref[...], down_ref[:, tile], preferred_element_type=F32) * scale_ref[:, :1]
        for n in range(2):
            begin = 2 * n * half
            refs[2 * n][:, tile] = out[begin : begin + half]
            refs[2 * n + 1][:, tile] = out[begin + half : begin + 2 * half].astype(BF16)


def add_kernel(kept_ref, got_ref, next_ref, sent_ref):
    half = next_ref.shape[0]
    total = kept_ref[...] + got_ref[...].astype(F32)
    next_ref[...] = total[:half]
    sent_ref[...] = total[half:].astype(BF16)


def close_kernel(kept_ref, *refs):
    total = kept_ref[...]
    for got_ref in refs[:-1]:
        total += got_ref[...].astype(F32)
    refs[-1][...] = total.astype(BF16)


def load(arrays, after):
    count, parts = len(arrays), 8

    def run(*refs):
        outs, sems = refs[count + len(after) : -1], refs[-1]
        copies = []
        for i in range(count):
            height = arrays[i].shape[0] // parts
            for n in range(parts):
                rows = pl.ds(n * height, height)
                copies.append(pltpu.make_async_copy(refs[i].at[rows], outs[i].at[rows], sems.at[i, n]))
        for copy in copies:
            copy.start()
        for copy in copies:
            copy.wait()

    return pl.pallas_call(
        run,
        out_shape=[pltpu.VMEM(a.shape, a.dtype) for a in arrays],
        in_specs=[HBM] * count + [ANY] * len(after),
        out_specs=[VMEM] * count,
        scratch_shapes=[pltpu.SemaphoreType.DMA((count, parts))],
        compiler_params=pltpu.CompilerParams(vmem_limit_bytes=MIB),
        cost_estimate=cost(4),
    )(*[pltpu.with_memory_space_constraint(a, pltpu.HBM) for a in arrays], *after)


def plan(experts):
    near, far = range(experts // 2), range(experts // 2, experts)
    steps = [("fetch", e) for e in sorted(range(1, experts), key=lambda e: (bin(e).count("1"), -e))]
    steps += [("behind", far[0])] + [("stack", e) for e in near]
    steps += [("behind", far[-1]), ("after", 0)] + [("stack", e) for e in far[:-1]]
    steps += [("behind", 1), ("stack", far[-1])]
    steps += [("load",)]
    steps += [("gate", (e, e + 1)) for e in near[::2]]
    steps += [("hold", far[-1], (near[-2], near[-1]))]
    steps += [("down", (e, e + 1)) for e in near[::2]]
    steps += [("gate", (e, e + 1)) for e in far[::2]]
    steps += [("down", (e, e + 1)) for e in far[::2][::-1]]
    back = range(experts)[::-1]
    steps += [("add1", e) for e in back]
    for slot in range(experts + 1):
        for step, lag in (("add2", 0), ("close", 1)):
            if 0 <= slot - lag < experts:
                steps.append((step, back[slot - lag]))
    return steps


def body(tokens, routes, route_weight, gate_weight, up_weight, down_weight):
    members = lax.axis_size("local")
    experts = members // SPLIT
    rows, features = tokens.shape
    hid = gate_weight.shape[2]

    width = -(-3 * experts // LANES) * LANES
    full = features + width
    sources = [tokens, routes.T, route_weight.T]
    payload = pl.pallas_call(
        functools.partial(pack_kernel, experts),
        out_shape=pltpu.VMEM((rows, full), BF16),
        in_specs=[HBM] * 3,
        out_specs=VMEM,
        scratch_shapes=[pltpu.VMEM(x.shape, x.dtype) for x in sources] + [pltpu.SemaphoreType.DMA((3,))],
        compiler_params=pltpu.CompilerParams(vmem_limit_bytes=MIB),
        cost_estimate=cost(0),
    )(*[pltpu.with_memory_space_constraint(x, pltpu.HBM) for x in sources])

    outer = {e: swap(members, lambda d, e=e: (e & -e) * SPLIT) for e in range(1, experts)}
    first = swap(members, lambda d: 4 if d & 1 else 2)
    second = swap(members, lambda d: 2 if d & 1 else 4)
    sibling = swap(members, lambda d: 1)
    mine = (lax.axis_index("local") // SPLIT).astype(jnp.int32)[None]
    weights = [gate_weight[0], up_weight[0], down_weight[0]]
    height = SPLIT * rows
    blocks, pairs, fars, nears = {0: payload}, {}, {}, {}
    hidden_of, state, home = {}, {}, []
    last = (payload,)
    for step, *at in plan(experts):
        e = at[0] if at else None
        if step == "fetch":
            blocks[e] = outer[e](blocks[e & (e - 1)])
            continue
        if step == "behind":
            last = (*last, blocks[e])
            continue
        if step == "after":
            last = (*last, fars[e])
            continue
        if step == "hold":
            fars[e], _ = lax.optimization_barrier((fars[e], hidden_of[at[1]][0]))
            continue
        if step == "stack":
            (out,) = call(stack_kernel, [shape(2 * rows, full, BF16)], [blocks[e], first(blocks[e])], last)
            pairs[e], fars[e], nears[e] = out, second(out), sibling(out)
        elif step == "load":
            weights = load(weights, last)
            out = weights[0]
        elif step == "gate":
            xs = [x for g in e for x in (pairs[g], fars[g], nears[g], sibling(fars[g]))]
            out, scale = pl.pallas_call(
                functools.partial(gate_kernel, len(xs), experts),
                out_shape=[pltpu.VMEM((2 * height, hid), BF16), pltpu.VMEM((2 * height, LANES), F32)],
                in_specs=[pl.BlockSpec(memory_space=pltpu.SMEM)] + [VMEM] * (len(xs) + 2) + [ANY] * len(last),
                out_specs=[VMEM, VMEM],
                compiler_params=pltpu.CompilerParams(vmem_limit_bytes=8 * MIB),
                cost_estimate=cost(2),
            )(mine, *xs, weights[0], weights[1], *last)
            hidden_of[e] = (out, scale)
        elif step == "down":
            half = height // 2
            made = call(
                down_kernel,
                [shape(half, features, t) for t in (F32, BF16, F32, BF16)],
                [*hidden_of[e], weights[2]],
                last,
            )
            out = made[-1]
            state[e[1]], state[e[0]] = (made[2], sibling(out)), (made[0], sibling(made[1]))
        elif step in ("add1", "add2"):
            kept, got = state[e]
            half = kept.shape[0] // 2
            kept, out = call(
                add_kernel, [shape(half, features, F32), shape(half, features, BF16)], [kept, got], last
            )
            state[e] = (kept, (second if step == "add1" else first)(out))
        else:
            (out,) = call(close_kernel, [shape(rows, features, BF16)], [*state[e], *(home if e == 0 else [])], last)
            if not e:
                return out
            home.append(swap(members, lambda d: e * SPLIT)(out))
        last = (out,)


def solution(mesh):
    return jax.shard_map(
        body,
        mesh=mesh,
        in_specs=(
            P(("parts", "local"), None),
            P(("parts", "local"), None),
            P(("parts", "local"), None),
            P("local", None, None),
            P("local", None, None),
            P("local", None, None),
        ),
        out_specs=P(("parts", "local"), None),
        check_vma=False,
    )
```

```python
import functools

import jax
import jax.numpy as jnp
from jax import lax
from jax.experimental import pallas as pl
from jax.experimental.pallas import tpu as pltpu
from jax.sharding import PartitionSpec as P

SPLIT = 8
LANES = 128
TILE = 512
MIB = 1 << 20
F32, BF16 = jnp.float32, jnp.bfloat16

VMEM = pl.BlockSpec(memory_space=pltpu.VMEM)
ANY = pl.BlockSpec(memory_space=pl.ANY)
HBM = pl.BlockSpec(memory_space=pltpu.HBM)


def cost(us):
    return pl.CostEstimate(flops=0, bytes_accessed=int(us * 3.6e6), transcendentals=0)


def swap(members, mask):
    pairs = [(d, d ^ mask(d)) for d in range(members)]
    return lambda x: lax.ppermute(x, "local", pairs)


def call(kernel, outs, operands, after=(), limit=8):
    count = len(operands)

    def run(*refs):
        kernel(*refs[:count], *refs[count + len(after) :])

    return pl.pallas_call(
        run,
        out_shape=[pltpu.VMEM(o.shape, o.dtype) for o in outs],
        in_specs=[VMEM] * count + [ANY] * len(after),
        out_specs=[VMEM] * len(outs),
        compiler_params=pltpu.CompilerParams(vmem_limit_bytes=limit * MIB),
        cost_estimate=cost(0),
    )(*operands, *after)


def shape(rows, columns, dtype):
    return jax.ShapeDtypeStruct((rows, columns), dtype)


def pack_kernel(experts, tokens_hbm, routes_hbm, weight_hbm, out_ref, tokens_ref, routes_ref, weight_ref, sems):
    rows, features = tokens_ref.shape
    copies = [
        pltpu.make_async_copy(routes_hbm, routes_ref, sems.at[0]),
        pltpu.make_async_copy(weight_hbm, weight_ref, sems.at[1]),
        pltpu.make_async_copy(tokens_hbm, tokens_ref, sems.at[2]),
    ]
    for copy in copies:
        copy.start()
    for copy in copies[:2]:
        copy.wait()
    width = out_ref.shape[1] - features
    column = lax.broadcasted_iota(jnp.int32, (rows, width), 1)
    square = (rows, rows)
    own = lax.broadcasted_iota(jnp.int32, square, 0) == lax.broadcasted_iota(jnp.int32, square, 1)
    coef = jnp.zeros((rows, width), F32)
    for k in range(routes_ref.shape[0]):
        route = jnp.sum(jnp.where(own, routes_ref[k : k + 1, :], 0), axis=1, keepdims=True)
        weight = jnp.sum(jnp.where(own, weight_ref[k : k + 1, :], 0.0), axis=1, keepdims=True)
        coef += jnp.where(lax.rem(column, experts) == route, weight, 0.0)
    high = coef.astype(BF16).astype(F32)
    middle = (coef - high).astype(BF16).astype(F32)
    low = coef - high - middle
    terms = jnp.where(column < experts, high, jnp.where(column < 2 * experts, middle, low))
    out_ref[:, features:] = jnp.where(column < 3 * experts, terms, 0.0).astype(BF16)
    copies[2].wait()
    out_ref[:, :features] = tokens_ref[...]


def stack_kernel(*refs):
    refs[-1][...] = jnp.concatenate([r[...] for r in refs[:-1]], axis=0)


def gate_kernel(pieces, experts, mine_ref, *refs):
    x_refs, (gate_ref, up_ref), (hidden_ref, scale_ref) = refs[:pieces], refs[pieces : pieces + 2], refs[-2:]
    features = gate_ref.shape[0]
    gate = up = jnp.zeros(hidden_ref.shape, F32)
    for lo in range(0, features, TILE):
        x = jnp.concatenate([r[:, lo : lo + TILE] for r in x_refs], axis=0)
        gate += jnp.dot(x, gate_ref[lo : lo + TILE, :], preferred_element_type=F32)
        up += jnp.dot(x, up_ref[lo : lo + TILE, :], preferred_element_type=F32)
    hidden_ref[...] = (jax.nn.silu(gate) * up).astype(BF16)
    terms = jnp.concatenate([r[:, features:] for r in x_refs], axis=0).astype(F32)
    column = lax.broadcasted_iota(jnp.int32, terms.shape, 1)
    wanted = (lax.rem(column, experts) == mine_ref[0]) & (column < 3 * experts)
    scale = jnp.sum(jnp.where(wanted, terms, 0.0), axis=1, keepdims=True)
    scale_ref[...] = jnp.broadcast_to(scale, scale_ref.shape)


def down_kernel(hidden_ref, scale_ref, down_ref, *refs):
    half, features = refs[0].shape
    for lo in range(0, features, TILE):
        tile = slice(lo, lo + TILE)
        out = jnp.dot(hidden_ref[...], down_ref[:, tile], preferred_element_type=F32) * scale_ref[:, :1]
        for n in range(2):
            begin = 2 * n * half
            refs[2 * n][:, tile] = out[begin : begin + half]
            refs[2 * n + 1][:, tile] = out[begin + half : begin + 2 * half].astype(BF16)


def add_kernel(kept_ref, got_ref, next_ref, sent_ref):
    half = next_ref.shape[0]
    total = kept_ref[...] + got_ref[...].astype(F32)
    next_ref[...] = total[:half]
    sent_ref[...] = total[half:].astype(BF16)


def close_kernel(kept_ref, *refs):
    total = kept_ref[...]
    for got_ref in refs[:-1]:
        total += got_ref[...].astype(F32)
    refs[-1][...] = total.astype(BF16)


def load(arrays, after):
    count, parts = len(arrays), 8

    def run(*refs):
        outs, sems = refs[count + len(after) : -1], refs[-1]
        copies = []
        for i in range(count):
            height = arrays[i].shape[0] // parts
            for n in range(parts):
                rows = pl.ds(n * height, height)
                copies.append(pltpu.make_async_copy(refs[i].at[rows], outs[i].at[rows], sems.at[i, n]))
        for copy in copies:
            copy.start()
        for copy in copies:
            copy.wait()

    return pl.pallas_call(
        run,
        out_shape=[pltpu.VMEM(a.shape, a.dtype) for a in arrays],
        in_specs=[HBM] * count + [ANY] * len(after),
        out_specs=[VMEM] * count,
        scratch_shapes=[pltpu.SemaphoreType.DMA((count, parts))],
        compiler_params=pltpu.CompilerParams(vmem_limit_bytes=MIB),
        cost_estimate=cost(4),
    )(*[pltpu.with_memory_space_constraint(a, pltpu.HBM) for a in arrays], *after)


def plan(experts):
    near, far = range(experts // 2), range(experts // 2, experts)
    steps = [("fetch", e) for e in sorted(range(1, experts), key=lambda e: (bin(e).count("1"), -e))]
    steps += [("behind", far[0])] + [("stack", e) for e in near]
    steps += [("behind", far[-1]), ("after", 0)] + [("stack", e) for e in far[:-1]]
    steps += [("behind", 1), ("stack", far[-1])]
    steps += [("load",)]
    steps += [("gate", (e, e + 1)) for e in near[::2]]
    steps += [("hold", far[-1], (near[-2], near[-1]))]
    steps += [("down", (e, e + 1)) for e in near[::2]]
    steps += [("gate", (e, e + 1)) for e in far[::2]]
    steps += [("down", (e, e + 1)) for e in far[::2][::-1]]
    back = range(experts)[::-1]
    steps += [("add1", e) for e in back]
    for slot in range(experts + 1):
        for step, lag in (("add2", 0), ("close", 1)):
            if 0 <= slot - lag < experts:
                steps.append((step, back[slot - lag]))
    return steps


def body(tokens, routes, route_weight, gate_weight, up_weight, down_weight):
    members = lax.axis_size("local")
    experts = members // SPLIT
    rows, features = tokens.shape
    hid = gate_weight.shape[2]

    width = -(-3 * experts // LANES) * LANES
    full = features + width
    sources = [tokens, routes.T, route_weight.T]
    payload = pl.pallas_call(
        functools.partial(pack_kernel, experts),
        out_shape=pltpu.VMEM((rows, full), BF16),
        in_specs=[HBM] * 3,
        out_specs=VMEM,
        scratch_shapes=[pltpu.VMEM(x.shape, x.dtype) for x in sources] + [pltpu.SemaphoreType.DMA((3,))],
        compiler_params=pltpu.CompilerParams(vmem_limit_bytes=MIB),
        cost_estimate=cost(0),
    )(*[pltpu.with_memory_space_constraint(x, pltpu.HBM) for x in sources])

    outer = {e: swap(members, lambda d, e=e: (e & -e) * SPLIT) for e in range(1, experts)}
    first = swap(members, lambda d: 4 if d & 1 else 2)
    second = swap(members, lambda d: 2 if d & 1 else 4)
    sibling = swap(members, lambda d: 1)
    mine = (lax.axis_index("local") // SPLIT).astype(jnp.int32)[None]
    weights = [gate_weight[0], up_weight[0], down_weight[0]]
    height = SPLIT * rows
    blocks, pairs, fars, nears = {0: payload}, {}, {}, {}
    hidden_of, state, home = {}, {}, []
    last = (payload,)
    for step, *at in plan(experts):
        e = at[0] if at else None
        if step == "fetch":
            blocks[e] = outer[e](blocks[e & (e - 1)])
            continue
        if step == "behind":
            last = (*last, blocks[e])
            continue
        if step == "after":
            last = (*last, fars[e])
            continue
        if step == "hold":
            fars[e], _ = lax.optimization_barrier((fars[e], hidden_of[at[1]][0]))
            continue
        if step == "stack":
            (out,) = call(stack_kernel, [shape(2 * rows, full, BF16)], [blocks[e], first(blocks[e])], last)
            pairs[e], fars[e], nears[e] = out, second(out), sibling(out)
        elif step == "load":
            weights = load(weights, last)
            out = weights[0]
        elif step == "gate":
            xs = [x for g in e for x in (pairs[g], fars[g], nears[g], sibling(fars[g]))]
            out, scale = pl.pallas_call(
                functools.partial(gate_kernel, len(xs), experts),
                out_shape=[pltpu.VMEM((2 * height, hid), BF16), pltpu.VMEM((2 * height, LANES), F32)],
                in_specs=[pl.BlockSpec(memory_space=pltpu.SMEM)] + [VMEM] * (len(xs) + 2) + [ANY] * len(last),
                out_specs=[VMEM, VMEM],
                compiler_params=pltpu.CompilerParams(vmem_limit_bytes=8 * MIB),
                cost_estimate=cost(2),
            )(mine, *xs, weights[0], weights[1], *last)
            hidden_of[e] = (out, scale)
        elif step == "down":
            half = height // 2
            made = call(
                down_kernel,
                [shape(half, features, t) for t in (F32, BF16, F32, BF16)],
                [*hidden_of[e], weights[2]],
                last,
            )
            out = made[-1]
            state[e[1]], state[e[0]] = (made[2], sibling(out)), (made[0], sibling(made[1]))
        elif step in ("add1", "add2"):
            kept, got = state[e]
            half = kept.shape[0] // 2
            kept, out = call(
                add_kernel, [shape(half, features, F32), shape(half, features, BF16)], [kept, got], last
            )
            state[e] = (kept, (second if step == "add1" else first)(out))
        else:
            (out,) = call(close_kernel, [shape(rows, features, BF16)], [*state[e], *(home if e == 0 else [])], last)
            if not e:
                return out
            home.append(swap(members, lambda d: e * SPLIT)(out))
        last = (out,)


def solution(mesh):
    return jax.shard_map(
        body,
        mesh=mesh,
        in_specs=(
            P(("parts", "local"), None),
            P(("parts", "local"), None),
            P(("parts", "local"), None),
            P("local", None, None),
            P("local", None, None),
            P("local", None, None),
        ),
        out_specs=P(("parts", "local"), None),
        check_vma=False,
    )
```
